32 devices in a mesh: qrow: 4 (over x, core), qcol: 4 (over z), grp: 2 (over y).
Axes of the slice: x: 2, y: 2, z: 4, core: 2. Of those that a mesh axis runs over, the one named last changes fastest.
Arguments:
- density: float32 [512, 3, 128, 128], P(('qrow', 'qcol', 'grp')), may hold values from -1 to 1.5, as said below
- pattern: int32 [512, 3], P(('qrow', 'qcol', 'grp')), may hold values from 0 to 1, as said below
- qm_sites: float32 [4, 512], P(None, ('qrow', 'qcol', 'grp')), may hold values from 0 to 8, as said below
- positions: float32 [3, 8, 8, 4, 128], P(None, 'qrow', 'qcol', 'grp'), may hold values from 0 to 1
- atom_types: int32 [8, 8, 4, 128], P('qrow', 'qcol', 'grp'), may hold values from 0 to 7
- charges: float32 [8, 8, 4, 128], P('qrow', 'qcol', 'grp'), may hold values from -4 to 4
- eps_table: float32 [8], replicated, may hold values from 0.2 to 2
- embed_atoms: int32 [32, 32, 128], P(('qrow', 'qcol', 'grp')), may hold values from 0 to 1023
- embed_counts: int32 [32, 32], P(('qrow', 'qcol', 'grp')), may hold values from 0 to 128, as said below
Outputs:
- purified: float32 [512, 3, 128, 128], P(('qrow', 'qcol', 'grp'))
- mm_force: float32 [3, 8, 8, 4, 128], P(None, 'qrow', 'qcol', 'grp')
The draws below stay inside these ranges and needn't reach their ends.
Inputs may be any that keep to these rules, and one draw needn't show every extreme that they name: `pattern`: column 1 is 1 in every block row; column 0 is 1 in every block row i with i mod 16 < 1, and column 2 in every block row i with i mod 16 >= 15. `density`: dominant diagonal near 0.5 with small entries elsewhere. `qm_sites`: centres lie in the MM box; the fourth row lies in 0.2 to 0.8. `embed_counts`: one owner, drawn from the seed, receives 128 atoms from every device.
All inputs are finite; a program needn't handle non-finite values.
Results may differ from the reference program's by a relative error of at most 0.0003.
Values sent between devices are 32-bit elements; how exact they have to be, the bound alone decides.
A program may use at most 128 MiB of HBM per device.

```python
import math
import jax
import jax.numpy as jnp
from jax import lax

BS = 128
W = 1
NBAND = 3
RB = 16
NBLK = 512
ITERS = 6
CX = 2
CY = 2
CZ = 2
M = 128
NTYPE = 8
CAP = 128
ATOMS_DEV = 1024
NX = 8
NY = 8
NZ = 4
N_QROW = 4
N_QCOL = 4
N_GRP = 2
DEVICES = 32


def draw_density(key, part):
    full_shape = (NBLK, NBAND, BS, BS)
    noise_key, diag_key = jax.random.split(key)
    spread = 0.12 / math.sqrt(NBAND * BS)
    noise_part = spread * jax.random.normal(noise_key, full_shape, jnp.float32)
    levels = jax.random.uniform(diag_key, (NBLK, BS), jnp.float32, 0.45, 0.55)
    band_pick = (jnp.arange(NBAND) == W).astype(jnp.float32)
    identity = jnp.eye(BS, dtype=jnp.float32)
    return noise_part + band_pick[None, :, None, None] * identity[None, None] * levels[:, None, :, None]


def draw_pattern(key, part):
    coin_flips = jax.random.randint(key, (NBLK, NBAND), 0, 2, dtype=jnp.int32)
    columns = jnp.arange(NBAND, dtype=jnp.int32)[None, :]
    rows_in = (jnp.arange(NBLK, dtype=jnp.int32) % RB)[:, None]
    forced = (columns == W) | (columns == 0) & (rows_in < W) | (columns == NBAND - 1) & (rows_in >= RB - W)
    return jnp.where(forced, 1, coin_flips).astype(jnp.int32)


def draw_qm_sites(key, part):
    unit_draw = jax.random.uniform(key, (4, NBLK), jnp.float32)
    low_ends = jnp.array([0.0, 0.0, 0.0, 0.2], dtype=jnp.float32)
    span_list = jnp.array([NX, NY, NZ, 0.6], dtype=jnp.float32)
    return low_ends[:, None] + span_list[:, None] * unit_draw


def draw_embed_counts(key, part):
    hot_key, fill_key = jax.random.split(key)
    hottest = jax.random.randint(hot_key, (), 0, DEVICES, dtype=jnp.int32)
    load_draw = jax.random.randint(fill_key, (DEVICES, DEVICES), 0, CAP // 2 + 1, dtype=jnp.int32)
    columns = jnp.arange(DEVICES, dtype=jnp.int32)[None, :]
    return jnp.where(columns == hottest, CAP, load_draw).astype(jnp.int32)


def set_ends(result, stream_key, low, top_value):
    longest = result.shape.index(max(result.shape))
    spots = []
    for shift in (0, 1):
        where = [jax.random.randint(jax.random.fold_in(stream_key, axis), (), 0, length) for axis, length in enumerate(result.shape)]
        where[longest] = (where[longest] + shift) % result.shape[longest]
        spots.append(tuple(where))
    return result.at[spots[0]].set(low).at[spots[1]].set(top_value)


def block_scale(stream_key, dims, shards, low, top_value):
    factor_of, own = 1.0, jax.random.fold_in(stream_key, 6)
    for axis_at, blocks in shards:
        draws = jnp.exp(jax.random.uniform(jax.random.fold_in(own, axis_at), (blocks,), jnp.float32, low / len(shards), top_value / len(shards)))
        factor_of = factor_of * jnp.repeat(draws, dims[axis_at] // blocks).reshape([-1 if axis == axis_at else 1 for axis in range(len(dims))])
    return factor_of


def centred(stream_key, dims, width, most, shards=(), kind=jnp.bfloat16):
    values = jax.random.normal(stream_key, dims, jnp.float32) * width
    if len(shards) > 0:
        values = block_scale(stream_key, dims, shards, -0.22, 0.18) * values
    return jnp.clip(values, min=-most, max=most).astype(kind)


def setup_inputs(seed: int = 0) -> dict:
    keys = jax.random.split(jax.random.key(seed), 10)
    return {
        "density": draw_density(jax.random.fold_in(keys[9], 71), 0),
        "pattern": draw_pattern(jax.random.fold_in(keys[9], 71), 0),
        "qm_sites": draw_qm_sites(jax.random.fold_in(keys[9], 71), 0),
        "positions": jnp.clip(1.0 * jax.random.uniform(keys[3], (3, NX, NY, NZ, M), jnp.float32) ** block_scale(keys[3], (3, NX, NY, NZ, M), ((1, 4), (2, 4), (3, 2)), -0.2, 0.2), 0.0, 1.0),
        "atom_types": set_ends(jax.random.randint(keys[4], (NX, NY, NZ, M), 0, NTYPE), jax.random.fold_in(keys[4], 1), 0, NTYPE - 1).astype(jnp.int32),
        "charges": centred(keys[5], (NX, NY, NZ, M), 0.8, 4.0, ((0, 4), (1, 4), (2, 2)), jnp.float32),
        "eps_table": jnp.clip(jnp.exp(jax.random.uniform(keys[6], (NTYPE,), jnp.float32, math.log(0.2), math.log(2.0))), 0.2, 2.0),
        "embed_atoms": set_ends(jax.random.randint(keys[7], (DEVICES, DEVICES, CAP), 0, ATOMS_DEV), jax.random.fold_in(keys[7], 1), 0, ATOMS_DEV - 1).astype(jnp.int32),
        "embed_counts": draw_embed_counts(jax.random.fold_in(keys[9], 71), 0),
    }


SIGMA_SQ = 0.25
EMBED = 20.0
SOFTEN = 1.0

def keep_of(pattern, first_row, total_rows):
    row_ids = first_row + jnp.arange(pattern.shape[0], dtype=jnp.int32)[:, None]
    column_ids = row_ids + jnp.arange(pattern.shape[1], dtype=jnp.int32)[None, :] - W
    inside = (column_ids >= 0) & (column_ids < total_rows) & (pattern > 0)
    return jnp.where(inside, 1.0, 0.0).astype(jnp.float32)

def band_window(extended, row_count, half_band):
    width_band = 2 * half_band + 1
    window_rows = []
    for window_row in range(width_band):
        entries = []
        for target in range(width_band):
            offset = target - window_row + half_band
            block_piece = extended[window_row:window_row + row_count, min(max(offset, 0), width_band - 1)]
            if 0 <= offset < width_band:
                entries.append(block_piece)
            else:
                entries.append(jnp.zeros_like(block_piece))
        window_rows.append(jnp.stack(entries, axis=1))
    return jnp.stack(window_rows, axis=1)

def band_product(left_band, extended, keep_mask):
    row_count = left_band.shape[0]
    half_band = (left_band.shape[1] - 1) // 2
    window = band_window(extended, row_count, half_band)
    product = jnp.einsum('rapk,radkq->rdpq', left_band, window, precision=lax.Precision.HIGHEST)
    return product * keep_mask[:, :, None, None]

def reference_product(left_band, right_band, keep_mask):
    padded = jnp.pad(right_band, ((W, W), (0, 0), (0, 0), (0, 0)))

    def one_row(row_index):
        extended = lax.dynamic_slice_in_dim(padded, row_index, 2 * W + 1, 0)
        left_row = lax.dynamic_slice_in_dim(left_band, row_index, 1, 0)
        keep_row = lax.dynamic_slice_in_dim(keep_mask, row_index, 1, 0)
        return band_product(left_row, extended, keep_row)[0]
    return lax.map(one_row, jnp.arange(NBLK, dtype=jnp.int32))

def pair_force(own_cells, neighbour, offsets):
    delta_list = [own_cells[axis_id][..., :, None] - neighbour[axis_id][..., None, :] - offsets[axis_id] for axis_id in range(3)]
    distance_sq = delta_list[0] * delta_list[0] + delta_list[1] * delta_list[1] + delta_list[2] * delta_list[2]
    weight_pair = own_cells[3][..., :, None] * neighbour[3][..., None, :] * jnp.exp(-distance_sq / SIGMA_SQ)
    return jnp.stack([lax.optimization_barrier(jnp.sum(weight_pair * component, axis=-1)) for component in delta_list], axis=0)

def embed_term(coords, charge_row, centers, block_charge):
    gap_list = [coords[axis_id][:, None, :] - centers[axis_id][:, :, None] for axis_id in range(3)]
    total_sq = gap_list[0] * gap_list[0] + gap_list[1] * gap_list[1] + gap_list[2] * gap_list[2] + SOFTEN
    factor = block_charge[:, :, None] / (total_sq * jnp.sqrt(total_sq))
    return jnp.stack([EMBED * charge_row * lax.optimization_barrier(jnp.sum(factor * gap_part, axis=1)) for gap_part in gap_list], axis=0)

def by_device(field):
    components = field.shape[0]
    split_view = field.reshape(components, N_QROW, CX, N_QCOL, CY, N_GRP, CZ, M)
    return split_view.transpose(1, 3, 5, 0, 2, 4, 6, 7).reshape(N_QROW * N_QCOL * N_GRP, components, CX * CY * CZ * M)

def from_device(field):
    components = field.shape[1]
    split_view = field.reshape(N_QROW, N_QCOL, N_GRP, components, CX, CY, CZ, M)
    return split_view.transpose(3, 0, 4, 1, 5, 2, 6, 7).reshape(components, NX, NY, NZ, M)

def reference(density, pattern, qm_sites, positions, atom_types, charges, eps_table, embed_atoms, embed_counts):
    keep_mask = keep_of(pattern, 0, NBLK)
    current = density * keep_mask[:, :, None, None]
    for sweep_index in range(ITERS):
        square = reference_product(current, current, keep_mask)
        cube_term = reference_product(square, current, keep_mask)
        current = 3.0 * square - 2.0 * cube_term
    purified = current
    diag_mean = lax.optimization_barrier(jnp.mean(jnp.diagonal(current[:, W], axis1=1, axis2=2), axis=1))
    qm_charge = qm_sites[3] - diag_mean
    type_ids = jnp.arange(NTYPE, dtype=jnp.int32)[:, None, None, None, None]
    strength = jnp.sqrt(lax.optimization_barrier(jnp.sum(jnp.where(atom_types[None] == type_ids, eps_table[:, None, None, None, None], 0.0), axis=0)))
    stacked = jnp.concatenate([positions, strength[None]], axis=0)
    force_total = jnp.zeros_like(positions)
    for shift_x in (-1, 0, 1):
        for shift_y in (-1, 0, 1):
            for shift_z in (-1, 0, 1):
                neighbour = jnp.roll(stacked, (-shift_x, -shift_y, -shift_z), axis=(1, 2, 3))
                force_total = force_total + pair_force(stacked, neighbour, (shift_x, shift_y, shift_z))
    grid_shape = positions.shape[1:]
    coords = jnp.stack([positions[axis_id] + lax.broadcasted_iota(jnp.int32, grid_shape, axis_id).astype(jnp.float32) for axis_id in range(3)], axis=0)
    payload = by_device(jnp.concatenate([coords, charges[None]], axis=0))
    device_count = N_QROW * N_QCOL * N_GRP
    centers = qm_sites[:3].reshape(3, device_count, RB)
    owner_charge = qm_charge.reshape(device_count, RB)

    def per_source(inputs):
        rows_payload, atom_list, count_list = inputs
        chosen = jnp.take(rows_payload, atom_list, axis=1)
        live = jnp.arange(CAP, dtype=jnp.int32)[None, :] < count_list[:, None]
        charge_row = jnp.where(live, chosen[3], 0.0)
        force_rows = embed_term(chosen[:3], charge_row, centers, owner_charge)
        empty = jnp.zeros((3, rows_payload.shape[1]), jnp.float32)
        return empty.at[:, atom_list.reshape(-1)].add(force_rows.reshape(3, -1))
    embed_force = from_device(lax.map(per_source, (payload, embed_atoms, embed_counts)))
    return (purified, force_total + embed_force)
```

```python
import functools
import math

import jax
import jax.numpy as jnp
from jax import lax
from jax.experimental import pallas as pl
from jax.experimental.pallas import tpu as pltpu
from jax.sharding import PartitionSpec as P

W = 1
ITERS = 6


SIGMA_SQ = 0.25
EMBED = 20.0
SOFTEN = 1.0
MESH = pl.DeviceIdType.MESH
SCALE = math.sqrt(1.0 / (SIGMA_SQ * math.log(2.0)))


def split(value):
    high = value.astype(jnp.bfloat16)
    return high, (value - high.astype(jnp.float32)).astype(jnp.bfloat16)


def step_kernel(
    sizes, pattern_ref, eps_ref, counts_ref, density_ref, sites_ref, positions_ref, types_ref, charges_ref, lists_ref,
    out_ref, force_ref,
    z0, z1, high0, high1, low0, low1, edge0, edge1, edge_keep, keep_ref,
    keep_out, keep_in, first_out, first_in, third_out, third_in, outbox, inbox,
    blocks_ref, sites_in, site_rows, around_ref, spread, pair_ref, times_ref, field_ref,
    diag_ref, charge_out, charge_in, charge_square, charge_rows,
    send_sem, recv_sem, load_sem, store_sem, block_send, block_recv, site_send, site_recv, charge_send, charge_recv
):
    rows, bs = density_ref.shape[0], density_ref.shape[2]
    n_row, n_col, n_grp = sizes
    total = n_row * n_col * n_grp
    at_row, at_col, at_grp = lax.axis_index("qrow"), lax.axis_index("qcol"), lax.axis_index("grp")
    home = at_row * n_col + at_col
    me = home * n_grp + at_grp
    has_prev, has_next = me > 0, me < total - 1

    def place(index):
        return (index // (n_col * n_grp), (index // n_grp) % n_col, index % n_grp)

    to_prev, to_next = place(jnp.maximum(me - 1, 0)), place(jnp.minimum(me + 1, total - 1))
    targets, present = (to_prev, to_next), (has_prev, has_next)
    full, high, low, edge = (z0, z1), (high0, high1), (low0, low1), (edge0, edge1)

    def message(pair, number, side):
        source, landing = pair
        return pltpu.make_async_remote_copy(
            source.at[side], landing.at[1 - side], send_sem.at[number, side], recv_sem.at[number, 1 - side],
            device_id=targets[side], device_id_type=MESH)

    def level_boxes(level):
        return outbox.at[level], inbox.at[level]

    def send(pair, number):
        for side in range(2):
            @pl.when(present[side])
            def _():
                message(pair, number, side).start()

    def finish(pair, number, side):
        message(pair, number, side).wait_send()
        message(pair, number, 1 - side).wait_recv()

    barrier = pltpu.get_barrier_semaphore()

    def greet(k, carry):
        pl.semaphore_signal(barrier, inc=1, device_id=place(lax.rem(me + k, total)), device_id_type=MESH)
        return carry

    lax.fori_loop(1, total, greet, 0)

    near_rows, far_rows = (0, rows - 1), (1, rows - 2)
    loads = [pltpu.make_async_copy(density_ref.at[i], z0.at[i], load_sem.at[k]) for k, i in enumerate(near_rows + far_rows)]
    loads.append(pltpu.make_async_copy(density_ref.at[pl.ds(2, rows - 4)], z0.at[pl.ds(2, rows - 4)], load_sem.at[4]))
    for load in loads:
        load.start()

    def keep_row(i, carry):
        for e in range(3):
            column = me * rows + i + e - W
            inside = (column >= 0) & (column < total * rows) & (pattern_ref[i, e] > 0)
            keep_ref[i, e] = jnp.where(inside, 1.0, 0.0).astype(jnp.float32)
        return carry

    lax.fori_loop(0, rows, keep_row, 0)

    cells, atoms = charges_ref.shape
    kinds = types_ref[...]
    eps = jnp.zeros((cells, atoms), jnp.float32)
    for kind in range(eps_ref.shape[0]):
        eps = jnp.where(kinds == kind, eps_ref[kind], eps)
    strength = jnp.sqrt(eps)
    for axis in range(3):
        blocks_ref[4, at_grp, axis] = positions_ref[axis]
    blocks_ref[4, at_grp, 3] = jnp.log2(strength)
    blocks_ref[4, at_grp, 4] = jnp.zeros((8, atoms), jnp.float32)
    blocks_ref[4, at_grp, 4, 0:4, 0:rows] = sites_ref[...]

    eye = lax.broadcasted_iota(jnp.int32, (bs, bs), 0) == lax.broadcasted_iota(jnp.int32, (bs, bs), 1)
    half = jnp.where(eye, 0.5, 0.0)

    def put(slot, row, value):
        high[slot][row + 2], low[slot][row + 2] = split(value)

    def masked(i):
        blocks = [z0[i, e] if e == W else z0[i, e] * keep_ref[i, e] for e in range(3)]
        blocks[W] = blocks[W] - half
        for e in range(3):
            z0[i, e] = blocks[e]
        return jnp.concatenate(blocks, axis=1)

    for load in loads[:4]:
        load.wait()
    near = [masked(0), masked(rows - 1)]
    far = [masked(1), masked(rows - 2)]
    cut = (slice(0, 2 * bs), slice(bs, 3 * bs))
    rest = (slice(2 * bs, 3 * bs), slice(0, bs))
    for side in range(2):
        first_out[side] = near[side][:, cut[side]]
        third_out[side] = near[side][:, rest[side]]
        outbox[0, side] = far[side][:, cut[side]]
        for e in range(3):
            keep_out[side, e : e + 1, :] = jnp.full((1, bs), keep_ref[(rows - 1) * side, e], jnp.float32)

    pl.semaphore_wait(barrier, total - 1)
    send((first_out, first_in), 0)
    send(level_boxes(0), 3)
    send((third_out, third_in), 1)
    send((keep_out, keep_in), 2)

    across = pltpu.make_async_remote_copy(
        blocks_ref.at[4, at_grp], blocks_ref.at[4, at_grp], block_send.at[4], block_recv.at[4],
        device_id=(at_row, at_col, 1 - at_grp), device_id_type=MESH)
    across_in = pltpu.make_async_remote_copy(
        blocks_ref.at[4, 1 - at_grp], blocks_ref.at[4, 1 - at_grp], block_send.at[4], block_recv.at[4],
        device_id=(at_row, at_col, 1 - at_grp), device_id_type=MESH)
    across.start()

    for side, row in ((0, 0), (1, rows - 1)):
        put(0, row, near[side])
    for side, row in ((0, 1), (1, rows - 2)):
        put(0, row, far[side])
    blank = jnp.zeros((bs, 3 * bs), jnp.bfloat16)
    for side in range(2):
        edge_keep[side] = jnp.zeros((8, bs), jnp.float32)
        edge0[side] = jnp.zeros((bs, 3 * bs), jnp.float32)
        for slot in range(2):
            for row in ((0, 1), (rows + 2, rows + 3))[side]:
                high[slot][row] = blank
                low[slot][row] = blank

    loads[4].wait()

    def fill(i, carry):
        put(0, i, masked(i))
        return carry

    lax.fori_loop(2, rows - 2, fill, 0)

    def product(left_high, left_low, windows):
        parts = []
        for tile in range(2):
            columns = slice(tile * bs, (tile + 2) * bs)
            wide_high, wide_low = windows[tile]
            deep = jnp.concatenate([left_high[:, columns], left_low[:, columns], left_high[:, columns]], axis=1)
            wide = jnp.concatenate([wide_high, wide_high, wide_low], axis=0)
            parts.append(jnp.dot(deep, wide, preferred_element_type=jnp.float32))
        return [parts[0][:, :bs], parts[0][:, bs:] + parts[1][:, :bs], parts[1][:, bs:]]

    def window(store, i):
        before, here, after = store[i + 1], store[i + 2], store[i + 3]
        one = jnp.concatenate([before[:, bs:], here[:, : 2 * bs]], axis=0)
        none = jnp.zeros((bs, bs), jnp.bfloat16)
        top = jnp.concatenate([none, here[:, 2 * bs :]], axis=1)
        return one, jnp.concatenate([top, after[:, : 2 * bs]], axis=0)

    def own(i):
        return -1 < i < rows

    def masks(i):
        if own(i):
            return [keep_ref[i, e] for e in range(3)]
        return [edge_keep[0 if i < 0 else 1, e : e + 1, :] for e in range(3)]

    def squared(slot, i, factor, keep):
        windows = list(zip(window(high[slot], i), window(low[slot], i)))
        blocks = product(high[slot][i + 2], low[slot][i + 2], windows)
        blocks = [blocks[e] * (factor if e == W else keep[e] * factor) for e in range(3)]
        return split(jnp.concatenate(blocks, axis=1))

    def finished(slot, i, square, keep):
        windows = list(zip(window(high[slot], i), window(low[slot], i)))
        cube = product(square[0], square[1], windows)
        fresh = []
        for e in range(3):
            columns = slice(e * bs, (e + 1) * bs)
            old = full[slot][i, e] if own(i) else edge[slot][0 if i < 0 else 1, :, columns]
            fresh.append(old - (cube[e] if e == W else keep[e] * cube[e]))
            if own(i):
                full[1 - slot][i, e] = fresh[e]
            else:
                edge[1 - slot][0 if i < 0 else 1, :, columns] = fresh[e]
        put(1 - slot, i, jnp.concatenate(fresh, axis=1))

    def run(tasks):
        kept = [masks(i) for _, i, _ in tasks]
        squares = [squared(slot, i, factor, keep) for (slot, i, factor), keep in zip(tasks, kept)]
        for (slot, i, _), square, keep in zip(tasks, squares, kept):
            finished(slot, i, square, keep)

    middle = list(range(4, rows - 4))
    outer = [1, rows - 2, 2, rows - 3, 3, rows - 4]

    def factor_of(level):
        return (4.0 / 3.0) * 2.25**level

    def post(level, slot):
        for side, row in ((0, 1), (1, rows - 2)):
            for k, e in enumerate(((0, 1), (1, 2))[side]):
                outbox[level, side, :, k * bs : (k + 1) * bs] = full[slot][row, e]
        send(level_boxes(level), 3 + level)

    def take_far(level, slot):
        for side in range(2):
            @pl.when(present[side])
            def _():
                finish(level_boxes(level), 3 + level, side)
                row = (0, rows + 3)[side]
                columns = cut[1 - side]
                high[slot][row, :, columns], low[slot][row, :, columns] = split(inbox[level, side])

    def around_copy(k):
        step_row, step_col = k // 3 - 1, k % 3 - 1
        target = (lax.rem(at_row + step_row + n_row, n_row), lax.rem(at_col + step_col + n_col, n_col), at_grp)
        return pltpu.make_async_remote_copy(
            blocks_ref.at[4], blocks_ref.at[8 - k], block_send.at[k], block_recv.at[8 - k],
            device_id=target, device_id_type=MESH)

    def site_copy(k, slot):
        peer = lax.rem(home + k, n_row * n_col)
        where = home if slot is None else peer
        return pltpu.make_async_remote_copy(
            sites_in.at[where], sites_in.at[where], site_send.at[k], site_recv.at[where],
            device_id=(peer // n_col, lax.rem(peer, n_col), at_grp), device_id_type=MESH)

    others = [k for k in range(9) if k != 4]

    def pass_on():
        across.wait_send()
        across_in.wait_recv()
        for k in others:
            around_copy(k).start()
        for g in range(n_grp):
            sites_in[home, g] = blocks_ref[4, g, 4]

        def one(k, carry):
            site_copy(k, None).start()
            return carry

        lax.fori_loop(1, n_row * n_col, one, 0)

    def gather_around():
        for k in others:
            around_copy(k).wait_send()
            around_copy(8 - k).wait_recv()
        for x in range(-1, 3):
            for y in range(-1, 3):
                for z in range(-1, 3):
                    k = (x // 2 + 1) * 3 + y // 2 + 1
                    g = at_grp if 0 <= z < 2 else 1 - at_grp
                    cell = (x % 2) * 4 + (y % 2) * 2 + z % 2
                    at = (x + 1) * 16 + (y + 1) * 4 + z + 1
                    for axis, shift in enumerate((x, y, z)):
                        row = blocks_ref[k, g, axis, cell : cell + 1, :]
                        around_ref[axis, at : at + 1, :] = (row + float(shift)) * SCALE
                    around_ref[3, at : at + 1, :] = blocks_ref[k, g, 3, cell : cell + 1, :]

    def gather_sites():
        def one(k, carry):
            site_copy(k, None).wait_send()
            site_copy(k, k).wait_recv()
            return carry

        lax.fori_loop(1, n_row * n_col, one, 0)
        per = bs // 8

        def some(n, carry):
            tiles = sites_in[pl.ds(n * (per // n_grp), per // n_grp)].reshape(bs, atoms)
            turned = jnp.transpose(tiles)[:rows]
            for j in range(per):
                at = pl.ds(pl.multiple_of((n * per + j) * rows, rows), rows)
                for axis in range(3):
                    site_rows[axis, at, :] = jnp.broadcast_to(turned[:, j * 8 + axis : j * 8 + axis + 1], (rows, atoms))
            return carry

        lax.fori_loop(0, total // per, some, 0)

    def count_atoms():
        cell_ids = lax.broadcasted_iota(jnp.int32, (16, atoms), 0)
        atom_ids = lax.broadcasted_iota(jnp.int32, (atoms, atoms), 0)
        slot_ids = lax.broadcasted_iota(jnp.int32, (1, atoms), 1)
        shift = int(math.log2(atoms))

        def some(n, carry):
            for j in range(4):
                owner = n * 4 + j
                row = jnp.where(slot_ids < counts_ref[owner], lists_ref[pl.ds(owner, 1), :], -1)
                in_cell = jnp.where(cell_ids == (row >> shift), 1.0, 0.0).astype(jnp.bfloat16)
                in_slot = jnp.where(atom_ids == (row & (atoms - 1)), 1.0, 0.0).astype(jnp.bfloat16)
                times_ref[owner] = lax.dot_general(
                    in_cell, in_slot, (((1,), (1,)), ((), ())), preferred_element_type=jnp.float32)[:cells]
            return carry

        lax.fori_loop(0, total // 4, some, 0)

    def make_field():
        spot = [
            [positions_ref[axis, cell : cell + 1, :] + ((at_row, at_col, at_grp)[axis] * 2 + (cell >> (2 - axis)) % 2).astype(jnp.float32)
             for cell in range(cells)]
            for axis in range(3)
        ]

        def one(n, carry):
            at = pl.ds(pl.multiple_of(n * 8, 8), 8)
            site = [site_rows[axis, at, :] for axis in range(3)]
            times = times_ref[n // (rows // 8)]
            for cell in range(cells):
                gap = [spot[axis][cell] - site[axis] for axis in range(3)]
                square = gap[0] * gap[0] + gap[1] * gap[1] + gap[2] * gap[2] + SOFTEN
                root = lax.rsqrt(square)
                factor = times[cell : cell + 1, :] * (root * root * root)
                for axis in range(3):
                    field_ref[axis * cells + cell, at, :] = factor * gap[axis]
            return carry

        lax.fori_loop(0, total * rows // 8, one, 0)

    ones = jnp.ones((8, atoms), jnp.float32)
    group = 32

    def pair_cell(cell):
        corner = (cell // 4) * 16 + ((cell // 2) % 2) * 4 + cell % 2
        for axis in range(3):
            row = around_ref[axis, pl.ds(corner + 21, 1), :]
            spread[axis] = jnp.transpose(jnp.broadcast_to(row, (atoms, atoms)))

        def one_group(n, carry):
            here = pl.ds(pl.multiple_of(n * group, group), group)
            mine = [spread[axis, here, :] for axis in range(3)]
            sums = [jnp.zeros((group, atoms), jnp.float32) for _ in range(3)]
            for dx in range(3):
                for dy in range(3):
                    for dz in range(3):
                        at = pl.ds(corner + dx * 16 + dy * 4 + dz, 1)
                        gap = [mine[axis] - around_ref[axis, at, :] for axis in range(3)]
                        power = around_ref[3, at, :] - (gap[0] * gap[0] + gap[1] * gap[1] + gap[2] * gap[2])
                        weight = jnp.exp2(power)
                        sums = [sums[axis] + weight * gap[axis] for axis in range(3)]
            for axis in range(3):
                spread[3 + axis, here, :] = sums[axis]
            return carry

        lax.fori_loop(0, atoms // group, one_group, 0)
        for axis in range(3):
            summed = lax.dot_general(
                ones, spread[3 + axis], (((1,), (1,)), ((), ())),
                precision=lax.Precision.HIGHEST, preferred_element_type=jnp.float32)
            pair_ref[axis, pl.ds(cell, 1), :] = summed[:1]

    def pair_cells(low_cell, high_cell):
        def one(cell, carry):
            pair_cell(cell)
            return carry

        lax.fori_loop(low_cell, high_cell, one, 0)

    run([(0, i, factor_of(0)) for i in middle])
    run([(0, i, factor_of(0)) for i in outer])
    post(1, 1)
    pass_on()
    count_atoms()

    for side in range(2):
        @pl.when(present[side])
        def _():
            finish((first_out, first_in), 0, side)
            row = (1, rows + 2)[side]
            columns = cut[1 - side]
            edge0[side, :, columns] = first_in[side]
            high0[row, :, columns], low0[row, :, columns] = split(first_in[side])

    ends = [0, rows - 1]
    beyond = [-1, rows]
    run([(0, i, factor_of(0)) for i in ends] + [(1, i, factor_of(1)) for i in middle])
    gather_around()
    gather_sites()
    make_field()

    for side in range(2):
        @pl.when(present[side])
        def _():
            finish((third_out, third_in), 1, side)
            finish((keep_out, keep_in), 2, side)
            row = (1, rows + 2)[side]
            columns = rest[1 - side]
            edge0[side, :, columns] = third_in[side]
            high0[row, :, columns], low0[row, :, columns] = split(third_in[side])
            edge_keep[side] = keep_in[side]

    def two_levels(t, carry):
        for k in range(2):
            slot = 1 - k
            level = 2 + 2 * t + k
            now = jnp.where(t == 0, factor_of(1 + k), factor_of(3 + k))
            before = jnp.where(t == 0, factor_of(k), factor_of(2 + k))
            after = jnp.where(t == 0, factor_of(2 + k), factor_of(4 + k))
            take_far(level - 2, 1 - slot)
            run([(slot, i, now) for i in outer] + [(1 - slot, i, before) for i in beyond])

            @pl.when(level < ITERS - 1)
            def _():
                post(level, 1 - slot)

            run([(slot, i, now) for i in ends] + [(1 - slot, i, after) for i in middle])
            pair_cells(2 * (level - 2), 2 * (level - 2) + 2)
        return carry

    lax.fori_loop(0, ITERS // 2 - 1, two_levels, 0)

    def store(i):
        return pltpu.make_async_copy(z0.at[i], out_ref.at[i], store_sem.at[i])

    def complete(i):
        for e in range(3):
            block = z0[i, e] * (1.5**ITERS)
            if e == W:
                block = block + half
                diag_ref[pl.ds(i, 1), :] = jnp.sum(jnp.where(eye, block, 0.0), axis=0, keepdims=True)
            z0[i, e] = block
        store(i).start()

    last = factor_of(ITERS - 1)
    run([(1, i, last) for i in outer])

    def inner(i, carry):
        complete(i)
        return carry

    lax.fori_loop(1, rows - 1, inner, 0)
    charge_out[...] = jnp.zeros((1, atoms), jnp.float32)
    take_far(ITERS - 2, 0)
    run([(0, i, factor_of(ITERS - 2)) for i in beyond])
    run([(1, i, last) for i in ends])
    complete(0)
    complete(rows - 1)

    def charge_copy(k, slot):
        peer = lax.rem(me + k, total)
        return pltpu.make_async_remote_copy(
            charge_out, charge_in.at[me if slot is None else peer], charge_send.at[k],
            charge_recv.at[me if slot is None else peer], device_id=place(peer), device_id_type=MESH)

    means = lax.dot_general(
        ones, diag_ref[...], (((1,), (1,)), ((), ())),
        precision=lax.Precision.HIGHEST, preferred_element_type=jnp.float32)[:1] * (1.0 / bs)
    charge_out[:, 0:rows] = sites_ref[3:4, :] - means

    def tell(k, carry):
        charge_copy(k, None).start()
        return carry

    lax.fori_loop(1, total, tell, 0)
    charge_square[pl.ds(me, 1), :] = charge_out[...]

    def hear(k, carry):
        charge_copy(k, None).wait_send()
        charge_copy(k, k).wait_recv()
        peer = lax.rem(me + k, total)
        charge_square[pl.ds(peer, 1), :] = charge_in[peer]
        return carry

    lax.fori_loop(1, total, hear, 0)
    for n in range(0, total, bs):
        turned = jnp.transpose(charge_square[n : n + bs, :])[:rows]
        for j in range(min(bs, total - n)):
            at = (n + j) * rows
            charge_rows[at : at + rows, :] = jnp.broadcast_to(turned[:, j : j + 1], (rows, atoms))

    def add_up(n, sums):
        sums = list(sums)
        for part in range(4):
            at = pl.ds(pl.multiple_of(n * 32 + part * 8, 8), 8)
            charge = charge_rows[at, :]
            sums = [total_so_far + charge * field_ref[k, at, :] for k, total_so_far in enumerate(sums)]
        return tuple(sums)

    sums = lax.fori_loop(0, total * rows // 32, add_up, (jnp.zeros((8, atoms), jnp.float32),) * (3 * cells))
    own_strength = strength * (1.0 / SCALE)
    for axis in range(3):
        for cell in range(cells):
            force = jnp.sum(sums[axis * cells + cell], axis=0, keepdims=True)
            here = slice(cell, cell + 1)
            force_ref[axis, here, :] = (
                pair_ref[axis, here, :] * own_strength[here] + EMBED * charges_ref[here, :] * force)

    def drain(i, carry):
        store(i).wait()
        return carry

    lax.fori_loop(0, rows, drain, 0)


def step(pattern, eps, counts, density, sites, positions, types, charges, lists, sizes):
    rows, band, bs = density.shape[:3]
    cells, atoms = charges.shape
    total = sizes[0] * sizes[1] * sizes[2]
    vmem, smem, anywhere = (pl.BlockSpec(memory_space=space) for space in (pltpu.VMEM, pltpu.SMEM, pl.ANY))

    def f32(*shape):
        return pltpu.VMEM(shape, jnp.float32)

    two, one = f32(2, bs, 2 * bs), f32(2, bs, bs)
    level_box = f32(ITERS - 1, 2, bs, 2 * bs)
    parts = pltpu.VMEM((rows + 4, bs, band * bs), jnp.bfloat16)
    edges, keeps = f32(2, bs, band * bs), f32(2, 8, bs)

    def copies(*shape):
        return pltpu.SemaphoreType.DMA(shape)

    return pl.pallas_call(
        functools.partial(step_kernel, sizes),
        out_shape=(
            jax.ShapeDtypeStruct(density.shape, jnp.float32),
            jax.ShapeDtypeStruct((3, cells, atoms), jnp.float32),
        ),
        in_specs=[smem, smem, smem, anywhere, vmem, vmem, vmem, vmem, vmem],
        out_specs=(anywhere, vmem),
        scratch_shapes=[
            f32(*density.shape), f32(*density.shape), parts, parts, parts, parts, edges, edges, keeps,
            pltpu.SMEM((rows, band), jnp.float32),
            keeps, keeps, two, two, one, one, level_box, level_box,
            f32(9, 2, 5, cells, atoms), f32(total // 2, 2, 8, atoms), f32(3, total * rows, atoms),
            f32(4, 64, atoms), f32(6, atoms, atoms), f32(3, cells, atoms), f32(total, cells, atoms),
            f32(3 * cells, total * rows, atoms),
            f32(rows, bs), f32(1, atoms), f32(total, 1, atoms), f32(-(-total // bs) * bs, atoms), f32(total * rows, atoms),
            copies(ITERS + 2, 2), copies(ITERS + 2, 2), copies(5), copies(rows), copies(9), copies(9),
            copies(total // 2), copies(total // 2), copies(total), copies(total),
        ],
        compiler_params=pltpu.CompilerParams(
            collective_id=0, has_side_effects=True, vmem_limit_bytes=60 * 1024 * 1024
        ),
        cost_estimate=pl.CostEstimate(
            flops=2 * 3 * 8 * 2 * ITERS * rows * bs**3, bytes_accessed=8 * density.size,
            transcendentals=27 * cells * atoms * atoms
        ),
    )(pattern, eps, counts, density, sites, positions, types, charges, lists)


def per_device(
    density, pattern, qm_sites, positions, atom_types, charges, eps_table, embed_atoms, embed_counts
):
    sizes = tuple(lax.axis_size(axis) for axis in ("qrow", "qcol", "grp"))
    atoms = charges.shape[-1]
    purified, force = step(
        pattern, eps_table, embed_counts[0], density, qm_sites, positions.reshape(3, -1, atoms),
        atom_types.reshape(-1, atoms), charges.reshape(-1, atoms), embed_atoms[0], sizes
    )
    return purified, force.reshape(positions.shape)


def solution(mesh):
    in_specs = (
        P(("qrow", "qcol", "grp"), None, None, None),
        P(("qrow", "qcol", "grp"), None),
        P(None, ("qrow", "qcol", "grp")),
        P(None, "qrow", "qcol", "grp", None),
        P("qrow", "qcol", "grp", None),
        P("qrow", "qcol", "grp", None),
        P(),
        P(("qrow", "qcol", "grp"), None, None),
        P(("qrow", "qcol", "grp"), None),
    )
    out_specs = (P(("qrow", "qcol", "grp"), None, None, None), P(None, "qrow", "qcol", "grp", None))
    return jax.shard_map(
        per_device, mesh=mesh, in_specs=in_specs, out_specs=out_specs, check_vma=False
    )
```

```python
import functools
import math

import jax
import jax.numpy as jnp
from jax import lax
from jax.experimental import pallas as pl
from jax.experimental.pallas import tpu as pltpu
from jax.sharding import PartitionSpec as P

W = 1
ITERS = 6


SIGMA_SQ = 0.25
EMBED = 20.0
SOFTEN = 1.0
MESH = pl.DeviceIdType.MESH
EARLY_CELLS = 4
SCALE = math.sqrt(1.0 / (SIGMA_SQ * math.log(2.0)))


def split(value):
    high = value.astype(jnp.bfloat16)
    return high, (value - high.astype(jnp.float32)).astype(jnp.bfloat16)


def step_kernel(
    sizes, pattern_ref, eps_ref, counts_ref, density_ref, sites_ref, positions_in, types_in, charges_in, lists_in,
    z0, force_ref,
    positions_ref, types_ref, charges_ref, lists_ref, z1, high0, high1, low0, low1, edge0, edge1, edge_keep, keep_ref,
    keep_out, keep_in, first_out, first_in, third_out, third_in, outbox, inbox,
    blocks_ref, site_pair, sites_in, site_rows, around_ref, spread, pair_ref, times_ref, field_ref,
    diag_ref, charge_out, charge_in, charge_square, charge_rows,
    send_sem, recv_sem, load_sem, block_send, block_recv, site_send, site_recv, charge_send, charge_recv
):
    rows, bs = density_ref.shape[0], density_ref.shape[2]
    n_row, n_col, n_grp = sizes
    total = n_row * n_col * n_grp
    at_row, at_col, at_grp = lax.axis_index("qrow"), lax.axis_index("qcol"), lax.axis_index("grp")
    home = at_row * n_col + at_col
    me = home * n_grp + at_grp
    has_prev, has_next = me > 0, me < total - 1

    def place(index):
        return (index // (n_col * n_grp), (index // n_grp) % n_col, index % n_grp)

    to_prev, to_next = place(jnp.maximum(me - 1, 0)), place(jnp.minimum(me + 1, total - 1))
    targets, present = (to_prev, to_next), (has_prev, has_next)
    full, high, low, edge = (z0, z1), (high0, high1), (low0, low1), (edge0, edge1)

    def message(pair, number, side):
        source, landing = pair
        return pltpu.make_async_remote_copy(
            source.at[side], landing.at[1 - side], send_sem.at[number, side], recv_sem.at[number, 1 - side],
            device_id=targets[side], device_id_type=MESH)

    def level_boxes(level):
        return outbox.at[level], inbox.at[level]

    def send(pair, number):
        for side in range(2):
            @pl.when(present[side])
            def _():
                message(pair, number, side).start()

    def finish(pair, number, side):
        message(pair, number, side).wait_send()
        message(pair, number, 1 - side).wait_recv()

    barrier = pltpu.get_barrier_semaphore()

    def wrapped(value, count):
        return jnp.where(value >= count, value - count, value)

    def each_peer(act):
        def one(step_row, carry):
            for step_col in range(n_col):
                for step_grp in range(n_grp):
                    where = (wrapped(at_row + step_row, n_row), wrapped(at_col + step_col, n_col), wrapped(at_grp + step_grp, n_grp))
                    number = (step_row * n_col + step_col) * n_grp + step_grp
                    peer = (where[0] * n_col + where[1]) * n_grp + where[2]
                    if step_col == 0 and step_grp == 0:
                        @pl.when(step_row > 0)
                        def _():
                            act(number, peer, where)
                    else:
                        act(number, peer, where)
            return carry

        lax.fori_loop(0, n_row, one, 0)

    def greet(number, peer, where):
        pl.semaphore_signal(barrier, inc=1, device_id=where, device_id_type=MESH)

    each_peer(greet)

    near_rows, far_rows = (0, rows - 1), (1, rows - 2)
    loads = [pltpu.make_async_copy(density_ref.at[i], z0.at[i], load_sem.at[k]) for k, i in enumerate(near_rows + far_rows)]
    loads.append(pltpu.make_async_copy(density_ref.at[pl.ds(2, rows - 4)], z0.at[pl.ds(2, rows - 4)], load_sem.at[4]))
    small = ((positions_in, positions_ref), (types_in, types_ref), (charges_in, charges_ref), (lists_in, lists_ref))
    small = [pltpu.make_async_copy(*pair, load_sem.at[5 + k]) for k, pair in enumerate(small)]
    loads = loads[:4] + small + loads[4:]
    for load in loads:
        load.start()

    unit = lax.broadcasted_iota(jnp.int32, (rows, rows), 0) == lax.broadcasted_iota(jnp.int32, (rows, rows), 1)
    for e in range(3):
        column = me * rows + lax.broadcasted_iota(jnp.int32, (1, rows), 1) + e - W
        kept = jnp.where((column >= 0) & (column < total * rows) & (pattern_ref[e : e + 1, :] > 0), 1.0, 0.0)
        kept = jnp.sum(jnp.where(unit, jnp.broadcast_to(kept, (rows, rows)), 0.0), axis=1, keepdims=True)
        keep_ref[e] = jnp.broadcast_to(kept, (rows, bs))

    def keep_of(i, e):
        return keep_ref[e, pl.ds(i, 1), :]

    eye = lax.broadcasted_iota(jnp.int32, (bs, bs), 0) == lax.broadcasted_iota(jnp.int32, (bs, bs), 1)
    half = jnp.where(eye, 0.5, 0.0)

    def put(slot, row, value):
        high[slot][row + 2], low[slot][row + 2] = split(value)

    def masked(i):
        blocks = [z0[i, e] if e == W else z0[i, e] * keep_of(i, e) for e in range(3)]
        blocks[W] = blocks[W] - half
        for e in range(3):
            z0[i, e] = blocks[e]
        return jnp.concatenate(blocks, axis=1)

    for load in loads[:4]:
        load.wait()
    near = [masked(0), masked(rows - 1)]
    far = [masked(1), masked(rows - 2)]
    cut = (slice(0, 2 * bs), slice(bs, 3 * bs))
    rest = (slice(2 * bs, 3 * bs), slice(0, bs))
    for side in range(2):
        first_out[side] = near[side][:, cut[side]]
        third_out[side] = near[side][:, rest[side]]
        outbox[0, side] = far[side][:, cut[side]]
        for e in range(3):
            keep_out[side, e : e + 1, :] = keep_of((rows - 1) * side, e)

    pl.semaphore_wait(barrier, total - 1)
    send((first_out, first_in), 0)

    cells, atoms = charges_ref.shape
    for load in small:
        load.wait()
    kinds = types_ref[...]
    eps = jnp.zeros((cells, atoms), jnp.float32)
    for kind in range(eps_ref.shape[0]):
        eps = jnp.where(kinds == kind, eps_ref[kind], eps)
    strength = jnp.sqrt(eps)
    powers = jnp.log2(strength)
    for x in range(2):
        for y in range(2):
            pick = slice(4 * x + 2 * y, 4 * x + 2 * y + 2)
            tile = [positions_ref[axis, pick, :] for axis in range(3)] + [powers[pick]]
            blocks_ref[4, x, y, at_grp] = jnp.concatenate(tile, axis=0)
    site_pair[0] = jnp.zeros((8, atoms), jnp.float32)
    site_pair[0, :, 0:rows] = jnp.concatenate(
        [jnp.where(at_grp == g, sites_ref[...], 0.0) for g in range(n_grp)], axis=0)

    def across(g):
        return pltpu.make_async_remote_copy(
            blocks_ref.at[4, :, :, g], blocks_ref.at[4, :, :, g], block_send.at[4], block_recv.at[4],
            device_id=(at_row, at_col, 1 - at_grp), device_id_type=MESH)

    across_sites = pltpu.make_async_remote_copy(
        site_pair.at[0], site_pair.at[1], block_send.at[9], block_recv.at[9],
        device_id=(at_row, at_col, 1 - at_grp), device_id_type=MESH)
    across(at_grp).start()
    across_sites.start()

    for side, row in ((0, 0), (1, rows - 1)):
        put(0, row, near[side])
    for side, row in ((0, 1), (1, rows - 2)):
        put(0, row, far[side])
    blank = jnp.zeros((bs, 3 * bs), jnp.bfloat16)
    for side in range(2):
        edge_keep[side] = jnp.zeros((8, bs), jnp.float32)
        edge0[side] = jnp.zeros((bs, 3 * bs), jnp.float32)
        for slot in range(2):
            for row in ((0, 1), (rows + 2, rows + 3))[side]:
                high[slot][row] = blank
                low[slot][row] = blank

    loads[-1].wait()

    def fill(i, carry):
        put(0, i, masked(i))
        return carry

    lax.fori_loop(2, rows - 2, fill, 0)

    def product(left_high, left_low, windows):
        parts = []
        for tile in range(2):
            columns = slice(tile * bs, (tile + 2) * bs)
            wide_high, wide_low = windows[tile]
            deep = jnp.concatenate([left_high[:, columns], left_low[:, columns], left_high[:, columns]], axis=1)
            wide = jnp.concatenate([wide_high, wide_high, wide_low], axis=0)
            parts.append(jnp.dot(deep, wide, preferred_element_type=jnp.float32))
        return [parts[0][:, :bs], parts[0][:, bs:] + parts[1][:, :bs], parts[1][:, bs:]]

    def window(store, i):
        before, here, after = store[i + 1], store[i + 2], store[i + 3]
        one = jnp.concatenate([before[:, bs:], here[:, : 2 * bs]], axis=0)
        none = jnp.zeros((bs, bs), jnp.bfloat16)
        top = jnp.concatenate([none, here[:, 2 * bs :]], axis=1)
        return one, jnp.concatenate([top, after[:, : 2 * bs]], axis=0)

    def own(i):
        return -1 < i < rows

    def masks(i):
        if own(i):
            return [keep_of(i, e) for e in range(3)]
        return [edge_keep[0 if i < 0 else 1, e : e + 1, :] for e in range(3)]

    def squared(slot, i, factor, keep):
        windows = list(zip(window(high[slot], i), window(low[slot], i)))
        blocks = product(high[slot][i + 2], low[slot][i + 2], windows)
        blocks = [blocks[e] * (factor if e == W else keep[e] * factor) for e in range(3)]
        return split(jnp.concatenate(blocks, axis=1))

    def finished(slot, i, square, keep):
        windows = list(zip(window(high[slot], i), window(low[slot], i)))
        cube = product(square[0], square[1], windows)
        fresh = []
        for e in range(3):
            columns = slice(e * bs, (e + 1) * bs)
            old = full[slot][i, e] if own(i) else edge[slot][0 if i < 0 else 1, :, columns]
            fresh.append(old - (cube[e] if e == W else keep[e] * cube[e]))
            if own(i):
                full[1 - slot][i, e] = fresh[e]
            else:
                edge[1 - slot][0 if i < 0 else 1, :, columns] = fresh[e]
        put(1 - slot, i, jnp.concatenate(fresh, axis=1))

    def run(tasks):
        kept = [masks(i) for _, i, _ in tasks]
        squares = [squared(slot, i, factor, keep) for (slot, i, factor), keep in zip(tasks, kept)]
        for (slot, i, _), square, keep in zip(tasks, squares, kept):
            finished(slot, i, square, keep)

    middle = list(range(4, rows - 4))
    outer = [1, rows - 2, 2, rows - 3, 3, rows - 4]

    def factor_of(level):
        return (4.0 / 3.0) * 2.25**level

    def post(level, slot):
        for side, row in ((0, 1), (1, rows - 2)):
            for k, e in enumerate(((0, 1), (1, 2))[side]):
                outbox[level, side, :, k * bs : (k + 1) * bs] = full[slot][row, e]
        send(level_boxes(level), 3 + level)

    def take_far(level, slot):
        for side in range(2):
            @pl.when(present[side])
            def _():
                finish(level_boxes(level), 3 + level, side)
                row = (0, rows + 3)[side]
                columns = cut[1 - side]
                high[slot][row, :, columns], low[slot][row, :, columns] = split(inbox[level, side])

    def around_copy(k):
        step_row, step_col = k // 3 - 1, k % 3 - 1
        target = (lax.rem(at_row + step_row + n_row, n_row), lax.rem(at_col + step_col + n_col, n_col), at_grp)
        xs, ys = ((pl.ds(0, 1), pl.ds(0, 2), pl.ds(1, 1))[step + 1] for step in (step_row, step_col))
        return pltpu.make_async_remote_copy(
            blocks_ref.at[4, xs, ys], blocks_ref.at[8 - k, xs, ys], block_send.at[k], block_recv.at[8 - k],
            device_id=target, device_id_type=MESH)

    def site_copy(k, slot):
        peer = lax.rem(home + k, n_row * n_col)
        where = home if slot is None else peer
        return pltpu.make_async_remote_copy(
            sites_in.at[where], sites_in.at[where], site_send.at[k], site_recv.at[where],
            device_id=(peer // n_col, lax.rem(peer, n_col), at_grp), device_id_type=MESH)

    others = [k for k in range(9) if k != 4]

    def pass_on():
        across(at_grp).wait_send()
        across(1 - at_grp).wait_recv()
        across_sites.wait()
        for k in others:
            around_copy(k).start()
        sites_in[home] = site_pair[0] + site_pair[1]

        def one(k, carry):
            site_copy(k, None).start()
            return carry

        lax.fori_loop(1, n_row * n_col, one, 0)

    def gather_around():
        for k in others:
            around_copy(k).wait_send()
            around_copy(8 - k).wait_recv()
        for x in range(-1, 3):
            for y in range(-1, 3):
                for z in range(-1, 3):
                    k = (x // 2 + 1) * 3 + y // 2 + 1
                    g = at_grp if 0 <= z < 2 else 1 - at_grp
                    at = (x + 1) * 16 + (y + 1) * 4 + z + 1
                    tile = blocks_ref.at[k, x % 2, y % 2, g]
                    for axis, shift in enumerate((x, y, z)):
                        from_row = 2 * axis + z % 2
                        around_ref[axis, at : at + 1, :] = (tile[from_row : from_row + 1, :] + float(shift)) * SCALE
                    around_ref[3, at : at + 1, :] = tile[6 + z % 2 : 7 + z % 2, :]

    def gather_sites():
        def one(k, carry):
            site_copy(k, None).wait_send()
            site_copy(k, k).wait_recv()
            return carry

        lax.fori_loop(1, n_row * n_col, one, 0)
        per = bs // 4

        def some(n, carry):
            tiles = sites_in[pl.ds(n * (per // 2), per // 2)].reshape(bs, atoms)
            turned = jnp.transpose(tiles)[:rows]
            for j in range(per):
                at = pl.ds(pl.multiple_of((n * per + j) * rows, rows), rows)
                for axis in range(3):
                    site_rows[axis, at, :] = jnp.broadcast_to(turned[:, j * 4 + axis : j * 4 + axis + 1], (rows, atoms))
            return carry

        lax.fori_loop(0, total // per, some, 0)

    def count_atoms():
        cell_ids = lax.broadcasted_iota(jnp.int32, (16, atoms), 0)
        atom_ids = lax.broadcasted_iota(jnp.int32, (atoms, atoms), 0)
        slot_ids = lax.broadcasted_iota(jnp.int32, (1, atoms), 1)
        shift = int(math.log2(atoms))

        def some(n, carry):
            for j in range(4):
                owner = n * 4 + j
                row = jnp.where(slot_ids < counts_ref[owner], lists_ref[pl.ds(owner, 1), :], -1)
                in_cell = jnp.where(cell_ids == (row >> shift), 1.0, 0.0).astype(jnp.bfloat16)
                in_slot = jnp.where(atom_ids == (row & (atoms - 1)), 1.0, 0.0).astype(jnp.bfloat16)
                times_ref[owner] = lax.dot_general(
                    in_cell, in_slot, (((1,), (1,)), ((), ())), preferred_element_type=jnp.float32)[:cells]
            return carry

        lax.fori_loop(0, total // 4, some, 0)

    def make_field():
        spot = [
            [positions_ref[axis, cell : cell + 1, :] + ((at_row, at_col, at_grp)[axis] * 2 + (cell >> (2 - axis)) % 2).astype(jnp.float32)
             for cell in range(cells)]
            for axis in range(3)
        ]

        def one(n, carry):
            at = pl.ds(pl.multiple_of(n * 8, 8), 8)
            site = [site_rows[axis, at, :] for axis in range(3)]
            times = times_ref[n // (rows // 8)]
            for cell in range(cells):
                gap = [spot[axis][cell] - site[axis] for axis in range(3)]
                square = gap[0] * gap[0] + gap[1] * gap[1] + gap[2] * gap[2] + SOFTEN
                root = lax.rsqrt(square)
                factor = times[cell : cell + 1, :] * (root * root * root)
                for axis in range(3):
                    field_ref[axis * cells + cell, at, :] = factor * gap[axis]
            return carry

        lax.fori_loop(0, total * rows // 8, one, 0)

    ones = jnp.ones((8, atoms), jnp.float32)
    group = 32

    def pair_cell(cell):
        corner = (cell // 4) * 16 + ((cell // 2) % 2) * 4 + cell % 2
        for axis in range(3):
            row = around_ref[axis, pl.ds(corner + 21, 1), :]
            spread[axis] = jnp.transpose(jnp.broadcast_to(row, (atoms, atoms)))

        def one_group(n, carry):
            here = pl.ds(pl.multiple_of(n * group, group), group)
            mine = [spread[axis, here, :] for axis in range(3)]
            sums = [jnp.zeros((group, atoms), jnp.float32) for _ in range(3)]
            for dx in range(3):
                for dy in range(3):
                    for dz in range(3):
                        at = pl.ds(corner + dx * 16 + dy * 4 + dz, 1)
                        gap = [mine[axis] - around_ref[axis, at, :] for axis in range(3)]
                        power = around_ref[3, at, :] - (gap[0] * gap[0] + gap[1] * gap[1] + gap[2] * gap[2])
                        weight = jnp.exp2(power)
                        sums = [sums[axis] + weight * gap[axis] for axis in range(3)]
            for axis in range(3):
                spread[3 + axis, here, :] = sums[axis]
            return carry

        lax.fori_loop(0, atoms // group, one_group, 0)
        for axis in range(3):
            summed = lax.dot_general(
                ones, spread[3 + axis], (((1,), (1,)), ((), ())),
                precision=lax.Precision.HIGHEST, preferred_element_type=jnp.float32)
            pair_ref[axis, pl.ds(cell, 1), :] = summed[:1]

    def pair_cells(low_cell, high_cell):
        def one(cell, carry):
            pair_cell(cell)
            return carry

        lax.fori_loop(low_cell, high_cell, one, 0)

    run([(0, i, factor_of(0)) for i in middle])
    send(level_boxes(0), 3)
    send((third_out, third_in), 1)
    send((keep_out, keep_in), 2)
    run([(0, i, factor_of(0)) for i in outer])
    post(1, 1)
    pass_on()
    count_atoms()

    for side in range(2):
        @pl.when(present[side])
        def _():
            finish((first_out, first_in), 0, side)
            row = (1, rows + 2)[side]
            columns = cut[1 - side]
            edge0[side, :, columns] = first_in[side]
            high0[row, :, columns], low0[row, :, columns] = split(first_in[side])

    ends = [0, rows - 1]
    beyond = [-1, rows]
    run([(0, i, factor_of(0)) for i in ends] + [(1, i, factor_of(1)) for i in middle])
    gather_around()
    gather_sites()
    make_field()

    for side in range(2):
        @pl.when(present[side])
        def _():
            finish((third_out, third_in), 1, side)
            finish((keep_out, keep_in), 2, side)
            row = (1, rows + 2)[side]
            columns = rest[1 - side]
            edge0[side, :, columns] = third_in[side]
            high0[row, :, columns], low0[row, :, columns] = split(third_in[side])
            edge_keep[side] = keep_in[side]

    def two_levels(t, carry):
        for k in range(2):
            slot = 1 - k
            level = 2 + 2 * t + k
            now = jnp.where(t == 0, factor_of(1 + k), factor_of(3 + k))
            before = jnp.where(t == 0, factor_of(k), factor_of(2 + k))
            after = jnp.where(t == 0, factor_of(2 + k), factor_of(4 + k))
            take_far(level - 2, 1 - slot)
            run([(slot, i, now) for i in outer] + [(1 - slot, i, before) for i in beyond])

            @pl.when(level < ITERS - 1)
            def _():
                post(level, 1 - slot)

            run([(slot, i, now) for i in ends] + [(1 - slot, i, after) for i in middle])
            pair_cells(level - 2, level - 1)
        return carry

    lax.fori_loop(0, ITERS // 2 - 1, two_levels, 0)

    def complete(i):
        for e in range(3):
            block = z0[i, e] * (1.5**ITERS)
            if e == W:
                block = block + half
                diag_ref[pl.ds(i, 1), :] = jnp.sum(jnp.where(eye, block, 0.0), axis=0, keepdims=True)
            z0[i, e] = block

    last = factor_of(ITERS - 1)
    run([(1, i, last) for i in outer])

    def inner(i, carry):
        complete(i)
        return carry

    lax.fori_loop(1, rows - 1, inner, 0)
    charge_out[...] = jnp.zeros((1, atoms), jnp.float32)
    take_far(ITERS - 2, 0)
    run([(0, i, factor_of(ITERS - 2)) for i in beyond])
    run([(1, i, last) for i in ends])
    complete(0)
    complete(rows - 1)

    def charge_copy(number, slot, where):
        return pltpu.make_async_remote_copy(
            charge_out, charge_in.at[slot], charge_send.at[number], charge_recv.at[slot],
            device_id=where, device_id_type=MESH)

    means = lax.dot_general(
        ones, diag_ref[...], (((1,), (1,)), ((), ())),
        precision=lax.Precision.HIGHEST, preferred_element_type=jnp.float32)[:1] * (1.0 / bs)
    charge_out[:, 0:rows] = sites_ref[3:4, :] - means

    each_peer(lambda number, peer, where: charge_copy(number, me, where).start())
    charge_square[pl.ds(me, 1), :] = charge_out[...]
    pair_cells(EARLY_CELLS, cells)

    def hear(number, peer, where):
        charge_copy(number, me, where).wait_send()
        charge_copy(number, peer, where).wait_recv()
        charge_square[pl.ds(peer, 1), :] = charge_in[peer]

    each_peer(hear)
    for n in range(0, total, bs):
        turned = jnp.transpose(charge_square[n : n + bs, :])[:rows]
        for j in range(min(bs, total - n)):
            at = (n + j) * rows
            charge_rows[at : at + rows, :] = jnp.broadcast_to(turned[:, j : j + 1], (rows, atoms))

    def add_up(n, sums):
        sums = list(sums)
        for part in range(4):
            at = pl.ds(pl.multiple_of(n * 32 + part * 8, 8), 8)
            charge = charge_rows[at, :]
            sums = [total_so_far + charge * field_ref[k, at, :] for k, total_so_far in enumerate(sums)]
        return tuple(sums)

    sums = lax.fori_loop(0, total * rows // 32, add_up, (jnp.zeros((8, atoms), jnp.float32),) * (3 * cells))
    own_strength = strength * (1.0 / SCALE)
    for axis in range(3):
        for cell in range(cells):
            force = jnp.sum(sums[axis * cells + cell], axis=0, keepdims=True)
            here = slice(cell, cell + 1)
            force_ref[axis, here, :] = (
                pair_ref[axis, here, :] * own_strength[here] + EMBED * charges_ref[here, :] * force)


def step(pattern, eps, counts, density, sites, positions, types, charges, lists, sizes):
    rows, band, bs = density.shape[:3]
    cells, atoms = charges.shape
    total = sizes[0] * sizes[1] * sizes[2]
    vmem, smem, hbm = (pl.BlockSpec(memory_space=space) for space in (pltpu.VMEM, pltpu.SMEM, pltpu.HBM))

    def f32(*shape):
        return pltpu.VMEM(shape, jnp.float32)

    two, one = f32(2, bs, 2 * bs), f32(2, bs, bs)
    level_box = f32(ITERS - 1, 2, bs, 2 * bs)
    parts = pltpu.VMEM((rows + 4, bs, band * bs), jnp.bfloat16)
    edges, keeps = f32(2, bs, band * bs), f32(2, 8, bs)

    def copies(*shape):
        return pltpu.SemaphoreType.DMA(shape)

    return pl.pallas_call(
        functools.partial(step_kernel, sizes),
        out_shape=(
            jax.ShapeDtypeStruct(density.shape, jnp.float32),
            jax.ShapeDtypeStruct((3, cells, atoms), jnp.float32),
        ),
        in_specs=[vmem, smem, smem, hbm, vmem, hbm, hbm, hbm, hbm],
        out_specs=(vmem, vmem),
        scratch_shapes=[
            f32(*positions.shape), pltpu.VMEM(types.shape, jnp.int32), f32(*charges.shape), pltpu.VMEM(lists.shape, jnp.int32),
            f32(*density.shape), parts, parts, parts, parts, edges, edges, keeps,
            f32(band, rows, bs),
            keeps, keeps, two, two, one, one, level_box, level_box,
            f32(9, 2, 2, 2, 8, atoms), f32(2, 8, atoms), f32(total // 2, 8, atoms), f32(3, total * rows, atoms),
            f32(4, 64, atoms), f32(6, atoms, atoms), f32(3, cells, atoms), f32(total, cells, atoms),
            f32(3 * cells, total * rows, atoms),
            f32(rows, bs), f32(1, atoms), f32(total, 1, atoms), f32(-(-total // bs) * bs, atoms), f32(total * rows, atoms),
            copies(ITERS + 2, 2), copies(ITERS + 2, 2), copies(9), copies(10), copies(10),
            copies(total // 2), copies(total // 2), copies(total), copies(total),
        ],
        compiler_params=pltpu.CompilerParams(
            collective_id=0, has_side_effects=True, vmem_limit_bytes=26 * 1024 * 1024 + total * rows * atoms * 4 * (3 * cells + 4)
        ),
        cost_estimate=pl.CostEstimate(
            flops=2 * 3 * 8 * 2 * ITERS * rows * bs**3, bytes_accessed=8 * density.size,
            transcendentals=27 * cells * atoms * atoms
        ),
    )(*(pltpu.with_memory_space_constraint(x, pltpu.HBM) for x in (pattern, eps, counts, density, sites, positions, types, charges, lists)))


def per_device(
    density, pattern, qm_sites, positions, atom_types, charges, eps_table, embed_atoms, embed_counts
):
    sizes = tuple(lax.axis_size(axis) for axis in ("qrow", "qcol", "grp"))
    atoms = charges.shape[-1]
    purified, force = step(
        pattern.T, eps_table, embed_counts[0], density, qm_sites, positions.reshape(3, -1, atoms),
        atom_types.reshape(-1, atoms), charges.reshape(-1, atoms), embed_atoms[0], sizes
    )
    return purified, force.reshape(positions.shape)


def solution(mesh):
    in_specs = (
        P(("qrow", "qcol", "grp"), None, None, None),
        P(("qrow", "qcol", "grp"), None),
        P(None, ("qrow", "qcol", "grp")),
        P(None, "qrow", "qcol", "grp", None),
        P("qrow", "qcol", "grp", None),
        P("qrow", "qcol", "grp", None),
        P(),
        P(("qrow", "qcol", "grp"), None, None),
        P(("qrow", "qcol", "grp"), None),
    )
    out_specs = (P(("qrow", "qcol", "grp"), None, None, None), P(None, "qrow", "qcol", "grp", None))
    return jax.shard_map(
        per_device, mesh=mesh, in_specs=in_specs, out_specs=out_specs, check_vma=False
    )
```

```python
import functools
import math

import jax
import jax.numpy as jnp
from jax import lax
from jax.experimental import pallas as pl
from jax.experimental.pallas import tpu as pltpu
from jax.sharding import PartitionSpec as P

W = 1
ITERS = 6


SIGMA_SQ = 0.25
EMBED = 20.0
SOFTEN = 1.0
MESH = pl.DeviceIdType.MESH
EARLY_CELLS = 4
SCALE = math.sqrt(1.0 / (SIGMA_SQ * math.log(2.0)))


def split(value):
    high = value.astype(jnp.bfloat16)
    return high, (value - high.astype(jnp.float32)).astype(jnp.bfloat16)


def step_kernel(
    sizes, pattern_ref, eps_ref, counts_ref, density_ref, sites_ref, positions_in, types_in, charges_in, lists_in,
    z0, force_ref,
    positions_ref, types_ref, charges_ref, lists_ref, z1, high0, high1, low0, low1, edge0, edge1, edge_keep, keep_ref,
    keep_out, keep_in, first_out, first_in, third_out, third_in, outbox, inbox,
    blocks_ref, site_pair, sites_in, site_rows, around_ref, spread, pair_ref, times_ref, field_ref,
    diag_ref, charge_out, charge_in, charge_square, charge_rows,
    send_sem, recv_sem, load_sem, block_send, block_recv, site_send, site_recv, charge_send, charge_recv
):
    rows, bs = density_ref.shape[0], density_ref.shape[2]
    n_row, n_col, n_grp = sizes
    total = n_row * n_col * n_grp
    at_row, at_col, at_grp = lax.axis_index("qrow"), lax.axis_index("qcol"), lax.axis_index("grp")
    home = at_row * n_col + at_col
    me = home * n_grp + at_grp
    has_prev, has_next = me > 0, me < total - 1

    def place(index):
        return (index // (n_col * n_grp), (index // n_grp) % n_col, index % n_grp)

    to_prev, to_next = place(jnp.maximum(me - 1, 0)), place(jnp.minimum(me + 1, total - 1))
    targets, present = (to_prev, to_next), (has_prev, has_next)
    full, high, low, edge = (z0, z1), (high0, high1), (low0, low1), (edge0, edge1)

    def message(pair, number, side):
        source, landing = pair
        return pltpu.make_async_remote_copy(
            source.at[side], landing.at[1 - side], send_sem.at[number, side], recv_sem.at[number, 1 - side],
            device_id=targets[side], device_id_type=MESH)

    def level_boxes(level):
        return outbox.at[level], inbox.at[level]

    def send(pair, number):
        for side in range(2):
            @pl.when(present[side])
            def _():
                message(pair, number, side).start()

    def finish(pair, number, side):
        message(pair, number, side).wait_send()
        message(pair, number, 1 - side).wait_recv()

    barrier = pltpu.get_barrier_semaphore()

    def wrapped(value, count):
        return jnp.where(value >= count, value - count, value)

    def each_peer(act):
        def one(step_row, carry):
            for step_col in range(n_col):
                for step_grp in range(n_grp):
                    where = (wrapped(at_row + step_row, n_row), wrapped(at_col + step_col, n_col), wrapped(at_grp + step_grp, n_grp))
                    number = (step_row * n_col + step_col) * n_grp + step_grp
                    peer = (where[0] * n_col + where[1]) * n_grp + where[2]
                    if step_col == 0 and step_grp == 0:
                        @pl.when(step_row > 0)
                        def _():
                            act(number, peer, where)
                    else:
                        act(number, peer, where)
            return carry

        lax.fori_loop(0, n_row, one, 0)

    def greet(number, peer, where):
        pl.semaphore_signal(barrier, inc=1, device_id=where, device_id_type=MESH)

    each_peer(greet)

    near_rows, far_rows = (0, rows - 1), (1, rows - 2)
    loads = [pltpu.make_async_copy(density_ref.at[i], z0.at[i], load_sem.at[k]) for k, i in enumerate(near_rows + far_rows)]
    loads.append(pltpu.make_async_copy(density_ref.at[pl.ds(2, rows - 4)], z0.at[pl.ds(2, rows - 4)], load_sem.at[4]))
    small = ((positions_in, positions_ref), (types_in, types_ref), (charges_in, charges_ref), (lists_in, lists_ref))
    small = [pltpu.make_async_copy(*pair, load_sem.at[5 + k]) for k, pair in enumerate(small)]
    loads = loads[:4] + small + loads[4:]
    for load in loads:
        load.start()

    unit = lax.broadcasted_iota(jnp.int32, (rows, rows), 0) == lax.broadcasted_iota(jnp.int32, (rows, rows), 1)
    for e in range(3):
        column = me * rows + lax.broadcasted_iota(jnp.int32, (1, rows), 1) + e - W
        kept = jnp.where((column >= 0) & (column < total * rows) & (pattern_ref[e : e + 1, :] > 0), 1.0, 0.0)
        kept = jnp.sum(jnp.where(unit, jnp.broadcast_to(kept, (rows, rows)), 0.0), axis=1, keepdims=True)
        keep_ref[e] = jnp.broadcast_to(kept, (rows, bs))

    def keep_of(i, e):
        return keep_ref[e, pl.ds(i, 1), :]

    eye = lax.broadcasted_iota(jnp.int32, (bs, bs), 0) == lax.broadcasted_iota(jnp.int32, (bs, bs), 1)
    half = jnp.where(eye, 0.5, 0.0)

    def put(slot, row, value):
        high[slot][row + 2], low[slot][row + 2] = split(value)

    def masked(i):
        blocks = [z0[i, e] if e == W else z0[i, e] * keep_of(i, e) for e in range(3)]
        blocks[W] = blocks[W] - half
        for e in range(3):
            z0[i, e] = blocks[e]
        return jnp.concatenate(blocks, axis=1)

    for load in loads[:4]:
        load.wait()
    near = [masked(0), masked(rows - 1)]
    far = [masked(1), masked(rows - 2)]
    cut = (slice(0, 2 * bs), slice(bs, 3 * bs))
    rest = (slice(2 * bs, 3 * bs), slice(0, bs))
    for side in range(2):
        first_out[side] = near[side][:, cut[side]]
        third_out[side] = near[side][:, rest[side]]
        outbox[0, side] = far[side][:, cut[side]]
        for e in range(3):
            keep_out[side, e : e + 1, :] = keep_of((rows - 1) * side, e)

    pl.semaphore_wait(barrier, total - 1)
    send((first_out, first_in), 0)

    cells, atoms = charges_ref.shape
    for load in small:
        load.wait()
    kinds = types_ref[...]
    eps = jnp.zeros((cells, atoms), jnp.float32)
    for kind in range(eps_ref.shape[0]):
        eps = jnp.where(kinds == kind, eps_ref[kind], eps)
    strength = jnp.sqrt(eps)
    powers = jnp.log2(strength)
    for x in range(2):
        for y in range(2):
            pick = slice(4 * x + 2 * y, 4 * x + 2 * y + 2)
            tile = [positions_ref[axis, pick, :] for axis in range(3)] + [powers[pick]]
            blocks_ref[4, x, y, at_grp] = jnp.concatenate(tile, axis=0)
    site_pair[0] = jnp.zeros((8, atoms), jnp.float32)
    site_pair[0, :, 0:rows] = jnp.concatenate(
        [jnp.where(at_grp == g, sites_ref[...], 0.0) for g in range(n_grp)], axis=0)

    def across(g):
        return pltpu.make_async_remote_copy(
            blocks_ref.at[4, :, :, g], blocks_ref.at[4, :, :, g], block_send.at[4], block_recv.at[4],
            device_id=(at_row, at_col, 1 - at_grp), device_id_type=MESH)

    across_sites = pltpu.make_async_remote_copy(
        site_pair.at[0], site_pair.at[1], block_send.at[9], block_recv.at[9],
        device_id=(at_row, at_col, 1 - at_grp), device_id_type=MESH)
    across(at_grp).start()
    across_sites.start()

    for side, row in ((0, 0), (1, rows - 1)):
        put(0, row, near[side])
    for side, row in ((0, 1), (1, rows - 2)):
        put(0, row, far[side])
    blank = jnp.zeros((bs, 3 * bs), jnp.bfloat16)
    for side in range(2):
        edge_keep[side] = jnp.zeros((8, bs), jnp.float32)
        edge0[side] = jnp.zeros((bs, 3 * bs), jnp.float32)
        for slot in range(2):
            for row in ((0, 1), (rows + 2, rows + 3))[side]:
                high[slot][row] = blank
                low[slot][row] = blank

    loads[-1].wait()

    def fill(i, carry):
        put(0, i, masked(i))
        return carry

    lax.fori_loop(2, rows - 2, fill, 0)

    def product(left_high, left_low, windows):
        parts = []
        for tile in range(2):
            columns = slice(tile * bs, (tile + 2) * bs)
            wide_high, wide_low = windows[tile]
            deep = jnp.concatenate([left_high[:, columns], left_low[:, columns], left_high[:, columns]], axis=1)
            wide = jnp.concatenate([wide_high, wide_high, wide_low], axis=0)
            parts.append(jnp.dot(deep, wide, preferred_element_type=jnp.float32))
        return [parts[0][:, :bs], parts[0][:, bs:] + parts[1][:, :bs], parts[1][:, bs:]]

    def window(store, i):
        before, here, after = store[i + 1], store[i + 2], store[i + 3]
        one = jnp.concatenate([before[:, bs:], here[:, : 2 * bs]], axis=0)
        none = jnp.zeros((bs, bs), jnp.bfloat16)
        top = jnp.concatenate([none, here[:, 2 * bs :]], axis=1)
        return one, jnp.concatenate([top, after[:, : 2 * bs]], axis=0)

    def own(i):
        return -1 < i < rows

    def masks(i):
        if own(i):
            return [keep_of(i, e) for e in range(3)]
        return [edge_keep[0 if i < 0 else 1, e : e + 1, :] for e in range(3)]

    def squared(slot, i, factor, keep):
        windows = list(zip(window(high[slot], i), window(low[slot], i)))
        blocks = product(high[slot][i + 2], low[slot][i + 2], windows)
        blocks = [blocks[e] * (factor if e == W else keep[e] * factor) for e in range(3)]
        return split(jnp.concatenate(blocks, axis=1))

    def finished(slot, i, square, keep):
        windows = list(zip(window(high[slot], i), window(low[slot], i)))
        cube = product(square[0], square[1], windows)
        fresh = []
        for e in range(3):
            columns = slice(e * bs, (e + 1) * bs)
            old = full[slot][i, e] if own(i) else edge[slot][0 if i < 0 else 1, :, columns]
            fresh.append(old - (cube[e] if e == W else keep[e] * cube[e]))
            if own(i):
                full[1 - slot][i, e] = fresh[e]
            else:
                edge[1 - slot][0 if i < 0 else 1, :, columns] = fresh[e]
        put(1 - slot, i, jnp.concatenate(fresh, axis=1))

    def run(tasks):
        kept = [masks(i) for _, i, _ in tasks]
        squares = [squared(slot, i, factor, keep) for (slot, i, factor), keep in zip(tasks, kept)]
        for (slot, i, _), square, keep in zip(tasks, squares, kept):
            finished(slot, i, square, keep)

    middle = list(range(4, rows - 4))
    outer = [1, rows - 2, 2, rows - 3, 3, rows - 4]

    def factor_of(level):
        return (4.0 / 3.0) * 2.25**level

    def post(level, slot):
        for side, row in ((0, 1), (1, rows - 2)):
            for k, e in enumerate(((0, 1), (1, 2))[side]):
                outbox[level, side, :, k * bs : (k + 1) * bs] = full[slot][row, e]
        send(level_boxes(level), 3 + level)

    def take_far(level, slot):
        for side in range(2):
            @pl.when(present[side])
            def _():
                finish(level_boxes(level), 3 + level, side)
                row = (0, rows + 3)[side]
                columns = cut[1 - side]
                high[slot][row, :, columns], low[slot][row, :, columns] = split(inbox[level, side])

    def around_copy(k):
        step_row, step_col = k // 3 - 1, k % 3 - 1
        target = (lax.rem(at_row + step_row + n_row, n_row), lax.rem(at_col + step_col + n_col, n_col), at_grp)
        xs, ys = ((pl.ds(0, 1), pl.ds(0, 2), pl.ds(1, 1))[step + 1] for step in (step_row, step_col))
        return pltpu.make_async_remote_copy(
            blocks_ref.at[4, xs, ys], blocks_ref.at[8 - k, xs, ys], block_send.at[k], block_recv.at[8 - k],
            device_id=target, device_id_type=MESH)

    def site_copy(k, slot):
        peer = lax.rem(home + k, n_row * n_col)
        where = home if slot is None else peer
        return pltpu.make_async_remote_copy(
            sites_in.at[where], sites_in.at[where], site_send.at[k], site_recv.at[where],
            device_id=(peer // n_col, lax.rem(peer, n_col), at_grp), device_id_type=MESH)

    others = [k for k in range(9) if k != 4]

    def pass_on():
        across(at_grp).wait_send()
        across(1 - at_grp).wait_recv()
        across_sites.wait()
        for k in others:
            around_copy(k).start()
        sites_in[home] = site_pair[0] + site_pair[1]

        def one(k, carry):
            site_copy(k, None).start()
            return carry

        lax.fori_loop(1, n_row * n_col, one, 0)

    def gather_around():
        for k in others:
            around_copy(k).wait_send()
            around_copy(8 - k).wait_recv()
        for x in range(-1, 3):
            for y in range(-1, 3):
                for z in range(-1, 3):
                    k = (x // 2 + 1) * 3 + y // 2 + 1
                    g = at_grp if 0 <= z < 2 else 1 - at_grp
                    at = (x + 1) * 16 + (y + 1) * 4 + z + 1
                    tile = blocks_ref.at[k, x % 2, y % 2, g]
                    for axis, shift in enumerate((x, y, z)):
                        from_row = 2 * axis + z % 2
                        around_ref[axis, at : at + 1, :] = (tile[from_row : from_row + 1, :] + float(shift)) * SCALE
                    around_ref[3, at : at + 1, :] = tile[6 + z % 2 : 7 + z % 2, :]

    def gather_sites():
        def one(k, carry):
            site_copy(k, None).wait_send()
            site_copy(k, k).wait_recv()
            return carry

        lax.fori_loop(1, n_row * n_col, one, 0)
        per = bs // 4

        def some(n, carry):
            tiles = sites_in[pl.ds(n * (per // 2), per // 2)].reshape(bs, atoms)
            turned = jnp.transpose(tiles)[:rows]
            for j in range(per):
                at = pl.ds(pl.multiple_of((n * per + j) * rows, rows), rows)
                for axis in range(3):
                    site_rows[axis, at, :] = jnp.broadcast_to(turned[:, j * 4 + axis : j * 4 + axis + 1], (rows, atoms))
            return carry

        lax.fori_loop(0, total // per, some, 0)

    def count_atoms():
        cell_ids = lax.broadcasted_iota(jnp.int32, (16, atoms), 0)
        atom_ids = lax.broadcasted_iota(jnp.int32, (atoms, atoms), 0)
        slot_ids = lax.broadcasted_iota(jnp.int32, (1, atoms), 1)
        shift = int(math.log2(atoms))

        def some(n, carry):
            for j in range(4):
                owner = n * 4 + j
                row = jnp.where(slot_ids < counts_ref[owner], lists_ref[pl.ds(owner, 1), :], -1)
                in_cell = jnp.where(cell_ids == (row >> shift), 1.0, 0.0).astype(jnp.bfloat16)
                in_slot = jnp.where(atom_ids == (row & (atoms - 1)), 1.0, 0.0).astype(jnp.bfloat16)
                times_ref[owner] = lax.dot_general(
                    in_cell, in_slot, (((1,), (1,)), ((), ())), preferred_element_type=jnp.float32)[:cells]
            return carry

        lax.fori_loop(0, total // 4, some, 0)

    def make_field():
        spot = [
            [positions_ref[axis, cell : cell + 1, :] + ((at_row, at_col, at_grp)[axis] * 2 + (cell >> (2 - axis)) % 2).astype(jnp.float32)
             for cell in range(cells)]
            for axis in range(3)
        ]

        def one(n, carry):
            at = pl.ds(pl.multiple_of(n * 8, 8), 8)
            site = [site_rows[axis, at, :] for axis in range(3)]
            times = times_ref[n // (rows // 8)]
            for cell in range(cells):
                gap = [spot[axis][cell] - site[axis] for axis in range(3)]
                square = gap[0] * gap[0] + gap[1] * gap[1] + gap[2] * gap[2] + SOFTEN
                root = lax.rsqrt(square)
                factor = times[cell : cell + 1, :] * (root * root * root)
                for axis in range(3):
                    field_ref[axis * cells + cell, at, :] = factor * gap[axis]
            return carry

        lax.fori_loop(0, total * rows // 8, one, 0)

    ones = jnp.ones((8, atoms), jnp.float32)
    group = 32

    def pair_cell(cell):
        corner = (cell // 4) * 16 + ((cell // 2) % 2) * 4 + cell % 2
        for axis in range(3):
            row = around_ref[axis, pl.ds(corner + 21, 1), :]
            spread[axis] = jnp.transpose(jnp.broadcast_to(row, (atoms, atoms)))

        def one_group(n, carry):
            here = pl.ds(pl.multiple_of(n * group, group), group)
            mine = [spread[axis, here, :] for axis in range(3)]
            sums = [jnp.zeros((group, atoms), jnp.float32) for _ in range(3)]
            for dx in range(3):
                for dy in range(3):
                    for dz in range(3):
                        at = pl.ds(corner + dx * 16 + dy * 4 + dz, 1)
                        gap = [mine[axis] - around_ref[axis, at, :] for axis in range(3)]
                        power = around_ref[3, at, :] - (gap[0] * gap[0] + gap[1] * gap[1] + gap[2] * gap[2])
                        weight = jnp.exp2(power)
                        sums = [sums[axis] + weight * gap[axis] for axis in range(3)]
            for axis in range(3):
                spread[3 + axis, here, :] = sums[axis]
            return carry

        lax.fori_loop(0, atoms // group, one_group, 0)
        for axis in range(3):
            summed = lax.dot_general(
                ones, spread[3 + axis], (((1,), (1,)), ((), ())),
                precision=lax.Precision.HIGHEST, preferred_element_type=jnp.float32)
            pair_ref[axis, pl.ds(cell, 1), :] = summed[:1]

    def pair_cells(low_cell, high_cell):
        def one(cell, carry):
            pair_cell(cell)
            return carry

        lax.fori_loop(low_cell, high_cell, one, 0)

    run([(0, i, factor_of(0)) for i in middle])
    send(level_boxes(0), 3)
    send((third_out, third_in), 1)
    send((keep_out, keep_in), 2)
    run([(0, i, factor_of(0)) for i in outer])
    pass_on()
    count_atoms()

    for side in range(2):
        @pl.when(present[side])
        def _():
            finish((first_out, first_in), 0, side)
            row = (1, rows + 2)[side]
            columns = cut[1 - side]
            edge0[side, :, columns] = first_in[side]
            high0[row, :, columns], low0[row, :, columns] = split(first_in[side])

    post(1, 1)
    ends = [0, rows - 1]
    beyond = [-1, rows]
    run([(0, i, factor_of(0)) for i in ends] + [(1, i, factor_of(1)) for i in middle])
    gather_around()
    gather_sites()
    make_field()

    for side in range(2):
        @pl.when(present[side])
        def _():
            finish((third_out, third_in), 1, side)
            finish((keep_out, keep_in), 2, side)
            row = (1, rows + 2)[side]
            columns = rest[1 - side]
            edge0[side, :, columns] = third_in[side]
            high0[row, :, columns], low0[row, :, columns] = split(third_in[side])
            edge_keep[side] = keep_in[side]

    def two_levels(t, carry):
        for k in range(2):
            slot = 1 - k
            level = 2 + 2 * t + k
            now = jnp.where(t == 0, factor_of(1 + k), factor_of(3 + k))
            before = jnp.where(t == 0, factor_of(k), factor_of(2 + k))
            after = jnp.where(t == 0, factor_of(2 + k), factor_of(4 + k))
            run([(slot, i, now) for i in outer])

            @pl.when(level < ITERS - 1)
            def _():
                post(level, 1 - slot)

            pair_cells(level - 2, level - 1)
            take_far(level - 2, 1 - slot)
            run([(1 - slot, i, before) for i in beyond] + [(1 - slot, i, after) for i in middle[::2]])
            run([(slot, i, now) for i in ends] + [(1 - slot, i, after) for i in middle[1::2]])
        return carry

    lax.fori_loop(0, ITERS // 2 - 1, two_levels, 0)

    def complete(i):
        for e in range(3):
            block = z0[i, e] * (1.5**ITERS)
            if e == W:
                block = block + half
                diag_ref[pl.ds(i, 1), :] = jnp.sum(jnp.where(eye, block, 0.0), axis=0, keepdims=True)
            z0[i, e] = block

    last = factor_of(ITERS - 1)
    run([(1, i, last) for i in outer])

    def inner(i, carry):
        complete(i)
        return carry

    lax.fori_loop(1, rows - 1, inner, 0)
    charge_out[...] = jnp.zeros((1, atoms), jnp.float32)
    take_far(ITERS - 2, 0)
    run([(0, i, factor_of(ITERS - 2)) for i in beyond])
    run([(1, i, last) for i in ends])
    complete(0)
    complete(rows - 1)

    def charge_copy(number, slot, where):
        return pltpu.make_async_remote_copy(
            charge_out, charge_in.at[slot], charge_send.at[number], charge_recv.at[slot],
            device_id=where, device_id_type=MESH)

    means = lax.dot_general(
        ones, diag_ref[...], (((1,), (1,)), ((), ())),
        precision=lax.Precision.HIGHEST, preferred_element_type=jnp.float32)[:1] * (1.0 / bs)
    charge_out[:, 0:rows] = sites_ref[3:4, :] - means

    each_peer(lambda number, peer, where: charge_copy(number, me, where).start())
    charge_square[pl.ds(me, 1), :] = charge_out[...]
    pair_cells(EARLY_CELLS, cells)

    def hear(number, peer, where):
        charge_copy(number, me, where).wait_send()
        charge_copy(number, peer, where).wait_recv()
        charge_square[pl.ds(peer, 1), :] = charge_in[peer]

    each_peer(hear)
    for n in range(0, total, bs):
        turned = jnp.transpose(charge_square[n : n + bs, :])[:rows]
        for j in range(min(bs, total - n)):
            at = (n + j) * rows
            charge_rows[at : at + rows, :] = jnp.broadcast_to(turned[:, j : j + 1], (rows, atoms))

    def add_up(n, sums):
        sums = list(sums)
        for part in range(4):
            at = pl.ds(pl.multiple_of(n * 32 + part * 8, 8), 8)
            charge = charge_rows[at, :]
            sums = [total_so_far + charge * field_ref[k, at, :] for k, total_so_far in enumerate(sums)]
        return tuple(sums)

    sums = lax.fori_loop(0, total * rows // 32, add_up, (jnp.zeros((8, atoms), jnp.float32),) * (3 * cells))
    own_strength = strength * (1.0 / SCALE)
    for axis in range(3):
        for cell in range(cells):
            force = jnp.sum(sums[axis * cells + cell], axis=0, keepdims=True)
            here = slice(cell, cell + 1)
            force_ref[axis, here, :] = (
                pair_ref[axis, here, :] * own_strength[here] + EMBED * charges_ref[here, :] * force)


def step(pattern, eps, counts, density, sites, positions, types, charges, lists, sizes):
    rows, band, bs = density.shape[:3]
    cells, atoms = charges.shape
    total = sizes[0] * sizes[1] * sizes[2]
    vmem, smem, hbm = (pl.BlockSpec(memory_space=space) for space in (pltpu.VMEM, pltpu.SMEM, pltpu.HBM))

    def f32(*shape):
        return pltpu.VMEM(shape, jnp.float32)

    two, one = f32(2, bs, 2 * bs), f32(2, bs, bs)
    level_box = f32(ITERS - 1, 2, bs, 2 * bs)
    parts = pltpu.VMEM((rows + 4, bs, band * bs), jnp.bfloat16)
    edges, keeps = f32(2, bs, band * bs), f32(2, 8, bs)

    def copies(*shape):
        return pltpu.SemaphoreType.DMA(shape)

    return pl.pallas_call(
        functools.partial(step_kernel, sizes),
        out_shape=(
            jax.ShapeDtypeStruct(density.shape, jnp.float32),
            jax.ShapeDtypeStruct((3, cells, atoms), jnp.float32),
        ),
        in_specs=[vmem, smem, smem, hbm, vmem, hbm, hbm, hbm, hbm],
        out_specs=(vmem, vmem),
        scratch_shapes=[
            f32(*positions.shape), pltpu.VMEM(types.shape, jnp.int32), f32(*charges.shape), pltpu.VMEM(lists.shape, jnp.int32),
            f32(*density.shape), parts, parts, parts, parts, edges, edges, keeps,
            f32(band, rows, bs),
            keeps, keeps, two, two, one, one, level_box, level_box,
            f32(9, 2, 2, 2, 8, atoms), f32(2, 8, atoms), f32(total // 2, 8, atoms), f32(3, total * rows, atoms),
            f32(4, 64, atoms), f32(6, atoms, atoms), f32(3, cells, atoms), f32(total, cells, atoms),
            f32(3 * cells, total * rows, atoms),
            f32(rows, bs), f32(1, atoms), f32(total, 1, atoms), f32(-(-total // bs) * bs, atoms), f32(total * rows, atoms),
            copies(ITERS + 2, 2), copies(ITERS + 2, 2), copies(9), copies(10), copies(10),
            copies(total // 2), copies(total // 2), copies(total), copies(total),
        ],
        compiler_params=pltpu.CompilerParams(
            collective_id=0, has_side_effects=True, vmem_limit_bytes=26 * 1024 * 1024 + total * rows * atoms * 4 * (3 * cells + 4)
        ),
        cost_estimate=pl.CostEstimate(
            flops=2 * 3 * 8 * 2 * ITERS * rows * bs**3, bytes_accessed=8 * density.size,
            transcendentals=27 * cells * atoms * atoms
        ),
    )(*(pltpu.with_memory_space_constraint(x, pltpu.HBM) for x in (pattern, eps, counts, density, sites, positions, types, charges, lists)))


def per_device(
    density, pattern, qm_sites, positions, atom_types, charges, eps_table, embed_atoms, embed_counts
):
    sizes = tuple(lax.axis_size(axis) for axis in ("qrow", "qcol", "grp"))
    atoms = charges.shape[-1]
    purified, force = step(
        pattern.T, eps_table, embed_counts[0], density, qm_sites, positions.reshape(3, -1, atoms),
        atom_types.reshape(-1, atoms), charges.reshape(-1, atoms), embed_atoms[0], sizes
    )
    return purified, force.reshape(positions.shape)


def solution(mesh):
    in_specs = (
        P(("qrow", "qcol", "grp"), None, None, None),
        P(("qrow", "qcol", "grp"), None),
        P(None, ("qrow", "qcol", "grp")),
        P(None, "qrow", "qcol", "grp", None),
        P("qrow", "qcol", "grp", None),
        P("qrow", "qcol", "grp", None),
        P(),
        P(("qrow", "qcol", "grp"), None, None),
        P(("qrow", "qcol", "grp"), None),
    )
    out_specs = (P(("qrow", "qcol", "grp"), None, None, None), P(None, "qrow", "qcol", "grp", None))
    return jax.shard_map(
        per_device, mesh=mesh, in_specs=in_specs, out_specs=out_specs, check_vma=False
    )
```
